512 devices in a mesh: tm: 32 (over x, y), scen: 16 (over z, core).
Axes of the slice: x: 4, y: 8, z: 8, core: 2. Of those that a mesh axis runs over, the one named last changes fastest.
Arguments:
- closed_loop: float32 [1024, 96, 96], P('tm'), may hold values from -1 to 1
- gains: float32 [1024, 48, 96], P('tm'), may hold values from -0.625 to 0.625
- feedforward: float32 [1024, 48], P('tm'), may hold values from -6 to 6
- drift_terms: float32 [1024, 96], P('tm'), may hold values from -0.3 to 0.3
- initial_states: float32 [96, 1024], P(None, ('tm', 'scen')), may hold values from -6 to 6
Outputs:
- states: float32 [1024, 96, 1024], P(('tm', 'scen'))
- controls: float32 [1024, 48, 1024], P(('tm', 'scen'))
The draws below stay inside these ranges and needn't reach their ends.
All inputs are finite; a program needn't handle non-finite values.
Results may differ from the reference program's by a relative error of at most 0.0003.
Values sent between devices are 32-bit elements; how exact they have to be, the bound alone decides.
No kernel may reach another device: no remote copies, remote signals or barrier semaphores. Data moves between devices by JAX's collectives and lax.ppermute only.
A program may use at most 64 MiB of HBM per device.

```python
import math
import jax
import jax.numpy as jnp
from jax import lax

NX = 96
NU = 48
PERIOD_LENGTH = 1024
SCEN = 1024


def draw_closed_loop(key, part):
    draw_generator_bases = jax.random.split(jax.random.fold_in(key, 11), 7)
    sluggish_selector = jax.random.uniform(draw_generator_bases[0], (NX,)) < 0.5
    slow_scale = jnp.exp(jax.random.uniform(draw_generator_bases[1], (NX,), minval=math.log(3.0 * PERIOD_LENGTH), maxval=math.log(12.0 * PERIOD_LENGTH)))
    quick_scale = jnp.exp(jax.random.uniform(draw_generator_bases[2], (NX,), minval=math.log(15.0), maxval=math.log(40.0)))
    time_scale = jnp.where(sluggish_selector, slow_scale, quick_scale)
    random_perturbation = jnp.exp(jax.random.uniform(draw_generator_bases[3], (PERIOD_LENGTH, NX), minval=math.log(0.7), maxval=math.log(1.4)))
    decay_speeds = jnp.exp(-1.0 / (time_scale[None, :] * random_perturbation))
    spell_length_total = jax.random.randint(draw_generator_bases[4], (3,), 0, PERIOD_LENGTH)
    interval_persisting = jax.random.uniform(draw_generator_bases[5], (3,), minval=0.5, maxval=0.8)
    concordant_number = jnp.arange(PERIOD_LENGTH)[:, None] == spell_length_total[None, :]
    persistence_markers = jnp.prod(jnp.where(concordant_number, interval_persisting[None, :], 1.0), axis=1)
    decay_speeds = decay_speeds * jnp.where(sluggish_selector[None, :], persistence_markers[:, None], 1.0)
    noise = jax.random.normal(draw_generator_bases[6], (PERIOD_LENGTH, NX, NX), dtype=jnp.float32) * (0.18 / math.sqrt(NX))
    same_group = (sluggish_selector[:, None] == sluggish_selector[None, :]).astype(jnp.float32)
    skewed_portion = (noise - jnp.swapaxes(noise, 1, 2)) / math.sqrt(2.0) * same_group[None, :, :]
    identity_map = jnp.eye(NX, dtype=jnp.float32)[None, :, :]
    rotation = jnp.linalg.solve(identity_map - skewed_portion, identity_map + skewed_portion)
    return (decay_speeds[:, :, None] * rotation).astype(jnp.float32)


def level_of(rng, shape, shards, low, high):
    gain = 1.0
    for position, shards_of in shards:
        steps = jax.random.uniform(jax.random.fold_in(jax.random.fold_in(rng, 6), position), (shards_of,), jnp.float32, low / len(shards), high / len(shards))
        gain = gain * jnp.repeat(jnp.exp(steps), shape[position] // shards_of).reshape((-1,) + (1,) * (len(shape) - 1 - position))
    return gain


def centred(rng, shape, spread, reach, shards=(), kind=jnp.bfloat16):
    result = spread * jax.random.normal(rng, shape, jnp.float32)
    if shards:
        result = result * level_of(rng, shape, shards, -0.22, 0.18)
    return jnp.clip(result, -reach, reach).astype(kind)


def setup_inputs(seed: int = 0) -> dict:
    keys = jax.random.split(jax.random.key(seed), 6)
    closed_loop = draw_closed_loop(jax.random.fold_in(keys[5], 71), 0)
    gains = centred(keys[1], (PERIOD_LENGTH, NU, NX), NX ** -0.5, 0.625, ((0, 32),), jnp.float32)
    feedforward = centred(keys[2], (PERIOD_LENGTH, NU), 1.0, 6.0, ((0, 32),), jnp.float32)
    drift_terms = centred(keys[3], (PERIOD_LENGTH, NX), 0.05, 0.3, ((0, 32),), jnp.float32)
    initial_states = centred(keys[4], (NX, SCEN), 1.0, 6.0, ((1, 512),), jnp.float32)
    return dict(closed_loop=closed_loop, gains=gains, feedforward=feedforward, drift_terms=drift_terms, initial_states=initial_states)


def reference(closed_loop, gains, feedforward, drift_terms, initial_states):
    highest = lax.Precision.HIGHEST

    def advance(state, inputs):
        matrix, gain_rows, feed_term, drift_term = inputs
        control = feed_term[:, None] - jnp.dot(gain_rows.astype(jnp.float32), state.astype(jnp.float32), precision=highest, preferred_element_type=jnp.float32)
        next_state = jnp.dot(matrix.astype(jnp.float32), state.astype(jnp.float32), precision=highest, preferred_element_type=jnp.float32) + drift_term[:, None]
        return (next_state, (state, control))
    start = initial_states.astype(jnp.float32)
    _, (state_path, control_path) = lax.scan(advance, start, (closed_loop, gains, feedforward, drift_terms))
    return (jnp.transpose(state_path, (2, 1, 0)), jnp.transpose(control_path, (2, 1, 0)))
```

```python
import functools

import jax
import jax.numpy as jnp
from jax import lax
from jax.experimental import pallas as pl
from jax.experimental.pallas import tpu as pltpu
from jax.sharding import PartitionSpec as P

f32, bf16 = jnp.float32, jnp.bfloat16
LANES = 128
LIMIT = 40 * 1024 * 1024


def split(x):
    high = x.astype(bf16)
    return high, (x - high.astype(f32)).astype(bf16)


def dot(a, b):
    return jnp.dot(a, b, preferred_element_type=f32)


def dot_t(a, b):
    return lax.dot_general(a, b, (((1,), (1,)), ((), ())), preferred_element_type=f32)


def extended(x):
    n = x.shape[0]
    high, low = split(x)
    shape = (LANES - n, LANES)
    row, lane = (lax.broadcasted_iota(jnp.int32, shape, d) for d in (0, 1))
    one = jnp.where((row == 0) & (lane >= n), 1.0, 0.0).astype(bf16)
    return (
        jnp.concatenate([high, one], axis=0),
        jnp.concatenate([low, jnp.zeros(shape, bf16)], axis=0),
    )


def compose(later, earlier):
    lh, ll = split(later)
    eh, el = extended(earlier)
    return dot(lh, eh) + (dot(lh, el) + dot(ll, eh))


def carry(rows, following):
    rh, rl = split(rows)
    mh, ml = extended(following)
    return dot_t(rh, mh) + (dot_t(rh, ml) + dot_t(rl, mh))


def with_offset(matrix, offset):
    wide = jnp.broadcast_to(offset, (matrix.shape[0], LANES - matrix.shape[1]))
    return jnp.concatenate([matrix, wide], axis=1)


def rounds(read, levels, count):
    get = read
    for level in levels:
        count //= 2
        for k in range(count):
            level[k] = compose(get(2 * k + 1), get(2 * k))
        get = lambda k, level=level: level[k]
    return compose(get(1), get(0))


def summary_kernel(a_ref, d_ref, x_ref, out_ref, *rest):
    maps, levels = rest[0], rest[1:]
    steps, n = d_ref.shape
    offsets = jnp.transpose(d_ref[...])
    for t in range(steps):
        maps[t] = with_offset(a_ref[t], offsets[:, t : t + 1])
    total = rounds(lambda t: maps[t], levels, steps)
    tail = jnp.pad(x_ref[...], ((0, 6), (0, LANES - n)))
    for j in range(out_ref.shape[0]):
        out_ref[j, :n] = total
        out_ref[j, n:] = tail


def prefix_kernel(k_ref, f_ref, maps, l1, l2, l3, l4, high_ref, low_ref, rows_ref):
    steps, m, n = k_ref.shape
    feeds = jnp.transpose(f_ref[...])
    row, lane = (lax.broadcasted_iota(jnp.int32, (n, LANES), d) for d in (0, 1))
    unit = jnp.where(row == lane, 1.0, 0.0).astype(f32)
    levels = (maps, l1, l2, l3, l4)

    def put(t, value):
        rows_ref[pl.ds(t, n, stride=steps)] = value

    def get(t):
        return rows_ref[pl.ds(t, n, stride=steps)]

    put(0, unit)
    for depth in range(4, -1, -1):
        size = 1 << depth
        put(size, levels[depth][0])
        for t in range(2 * size, steps, 2 * size):
            put(t + size, compose(levels[depth][t // size], get(t)))
    for t in range(steps):
        gain = with_offset(-k_ref[t], feeds[:, t : t + 1])
        rows_ref[pl.ds(n * steps + t, m, stride=steps)] = compose(gain, get(t))
    block = 512
    for at in range(0, (n + m) * steps, block):
        high, low = split(rows_ref[at : at + block])
        high_ref[at : at + block] = high
        low_ref[at : at + block] = low


def group_kernel(r_ref, out_ref, l1, l2, l3):
    count, rows, _ = r_ref.shape
    n = rows - 8
    out_ref[:n] = rounds(lambda j: r_ref[j, :n], (l1, l2, l3), count)
    for s in range(2):
        for j in range(count):
            out_ref[n + s * count + j : n + s * count + j + 1] = r_ref[j, n + s : n + s + 1]


def inner_kernel(i_ref, r_ref, l1, l2, l3, out_ref):
    n = out_ref.shape[0]
    index = i_ref[0]
    row, lane = (lax.broadcasted_iota(jnp.int32, (n, LANES), d) for d in (0, 1))
    held = jnp.where(row == lane, 1.0, 0.0).astype(f32)
    held = jnp.where((index & 8) != 0, l3[0], held)
    for bit, read in (
        (4, lambda k: l2[k]),
        (2, lambda k: l1[k]),
        (1, lambda k: r_ref[k, :n]),
    ):
        at = (index // (2 * bit)) * 2
        held = jnp.where((index & bit) != 0, compose(read(at), held), held)
    out_ref[...] = held


def apply_kernel(i_ref, own_ref, other_ref, inner_ref, high_ref, low_ref, out_ref):
    n = inner_ref.shape[0]
    second = i_ref[0] >= 16
    own, other = own_ref[n:], other_ref[n:]
    halves = jnp.where(second, other, own), jnp.where(second, own, other)
    start = jnp.concatenate([h[16 * s : 16 * s + 16] for s in (0, 1) for h in halves], axis=0)
    lane = lax.broadcasted_iota(jnp.int32, start.shape, 1)
    start = jnp.where(lane < n, start, jnp.where(lane == n, 1.0, 0.0))
    start = jnp.where(second, carry(start, other_ref[:n]), start)
    xh, xl = split(carry(start, inner_ref[...]))
    count = high_ref.shape[0] // LANES
    first = count * 2 // 3
    rest = count - first
    for q in range(count):
        at = slice(q * LANES, (q + 1) * LANES)
        high = high_ref[at]
        value = dot_t(xh, high) + (dot_t(xl, high) + dot_t(xh, low_ref[at]))
        for s in (0, 1):
            line = s * first + q if q < first else 2 * first + s * rest + q - first
            out_ref[pl.ds(line, 32, stride=2 * count)] = value[32 * s : 32 * s + 32]


def order_kernel(r_ref, states_ref, controls_ref, tile_ref):
    lines = r_ref.shape[1]
    lane = lax.broadcasted_iota(jnp.int32, (lines, LANES), 1) // 32
    cut = states_ref.shape[0]
    for g in range(8):
        parts = [r_ref[4 * g + b] for b in range(4)]
        across = slice(g * LANES, (g + 1) * LANES)
        for a in range(4):
            value = None
            for b in range(4):
                moved = parts[b] if a == b else pltpu.roll(parts[b], 32 * ((b - a) % 4), 1)
                value = moved if value is None else jnp.where(lane == b, moved, value)
            tile_ref[pl.ds(g * 4 * lines + a, lines, stride=4)] = value
        base = g * 4 * lines
        states_ref[:, across] = tile_ref[base : base + cut]
        controls_ref[:, across] = tile_ref[base + cut : base + 4 * lines]


def call(kernel, outs, scratch=(), scalars=0, inputs=0, flops=0):
    vmem = pl.BlockSpec(memory_space=pltpu.VMEM)
    smem = pl.BlockSpec(memory_space=pltpu.SMEM)
    many = isinstance(outs, (list, tuple))
    return pl.pallas_call(
        kernel,
        out_shape=outs,
        in_specs=[smem] * scalars + [vmem] * inputs,
        out_specs=[vmem] * len(outs) if many else vmem,
        scratch_shapes=list(scratch),
        compiler_params=pltpu.CompilerParams(vmem_limit_bytes=LIMIT),
        cost_estimate=pl.CostEstimate(flops=flops, bytes_accessed=4000000, transcendentals=0),
    )


def body(closed_loop, gains, feedforward, drift_terms, initial_states):
    steps, n, _ = closed_loop.shape
    m = gains.shape[1]
    blocks = lax.axis_size("tm")
    half = blocks // 2
    shape = jax.ShapeDtypeStruct
    index = lax.axis_index("tm").astype(jnp.int32)
    inner_index = (index % half).reshape(1)
    index = index.reshape(1)

    def maps_of(count):
        return shape((count, n, LANES), f32)

    payload, *levels = call(
        summary_kernel,
        [shape((half, n + 8, LANES), f32)] + [maps_of(steps >> k) for k in range(5)],
        inputs=3,
        flops=300_000_000,
    )(closed_loop, drift_terms, jnp.transpose(initial_states))
    groups = [[h * half + j for j in range(half)] for h in range(2)]
    gathered = lax.all_to_all(payload, "tm", 0, 0, tiled=True, axis_index_groups=groups)

    high, low = call(
        prefix_kernel,
        [shape(((n + m) * steps, LANES), bf16)] * 2,
        scratch=[pltpu.VMEM(((n + m) * steps, LANES), f32)],
        inputs=7,
        flops=500_000_000,
    )(gains, feedforward, *levels)

    own, *group_levels = call(
        group_kernel,
        [shape((n + 2 * half, LANES), f32)] + [maps_of(half >> k) for k in (1, 2, 3)],
        inputs=1,
        flops=150_000_000,
    )(gathered)
    other = lax.ppermute(own, "tm", [(j, (j + half) % blocks) for j in range(blocks)])
    inner = call(
        inner_kernel, shape((n, LANES), f32), scalars=1, inputs=4, flops=50_000_000
    )(inner_index, gathered, *group_levels)

    lines = 2 * (n + m) * steps // LANES
    sent = call(
        apply_kernel,
        shape((blocks * lines, LANES), f32),
        scalars=1,
        inputs=5,
        flops=300_000_000,
    )(index, own, other, inner, high, low)
    moved = lax.all_to_all(sent.reshape(blocks, lines, LANES), "tm", 0, 0, tiled=True)
    states, controls = call(
        order_kernel,
        [shape((2 * n, blocks * steps), f32), shape((2 * m, blocks * steps), f32)],
        scratch=[pltpu.VMEM((8 * 4 * lines, LANES), f32)],
        inputs=1,
        flops=1_000_000,
    )(moved)
    return states.reshape(2, n, -1), controls.reshape(2, m, -1)


def solution(mesh):
    return jax.shard_map(
        body,
        mesh=mesh,
        in_specs=(
            P("tm", None, None),
            P("tm", None, None),
            P("tm", None),
            P("tm", None),
            P(None, ("tm", "scen")),
        ),
        out_specs=(P(("tm", "scen"), None, None), P(("tm", "scen"), None, None)),
        check_vma=False,
    )
```

```python
import jax
import jax.numpy as jnp
from jax import lax
from jax.experimental import pallas as pl
from jax.experimental.pallas import tpu as pltpu
from jax.sharding import PartitionSpec as P

f32, bf16 = jnp.float32, jnp.bfloat16
LANES = 128
LIMIT = 40 * 1024 * 1024


def split(x):
    high = x.astype(bf16)
    return high, (x - high.astype(f32)).astype(bf16)


def dot(a, b):
    return jnp.dot(a, b, preferred_element_type=f32)


def dot_t(a, b):
    return lax.dot_general(a, b, (((1,), (1,)), ((), ())), preferred_element_type=f32)


def extended(x):
    n = x.shape[0]
    high, low = split(x)
    shape = (LANES - n, LANES)
    row, lane = (lax.broadcasted_iota(jnp.int32, shape, d) for d in (0, 1))
    one = jnp.where((row == 0) & (lane >= n), 1.0, 0.0).astype(bf16)
    return (
        jnp.concatenate([high, one], axis=0),
        jnp.concatenate([low, jnp.zeros(shape, bf16)], axis=0),
    )


def compose(later, earlier):
    lh, ll = split(later)
    eh, el = extended(earlier)
    return dot(lh, eh) + (dot(lh, el) + dot(ll, eh))


def carry(rows, following):
    rh, rl = split(rows)
    mh, ml = extended(following)
    return dot_t(rh, mh) + (dot_t(rh, ml) + dot_t(rl, mh))


def with_offset(matrix, offset):
    wide = jnp.broadcast_to(offset, (matrix.shape[0], LANES - matrix.shape[1]))
    return jnp.concatenate([matrix, wide], axis=1)


def rounds(maps, count, at=0):
    while count > 2:
        end = at + count
        for k in range(count // 2):
            maps[end + k] = compose(maps[at + 2 * k + 1], maps[at + 2 * k])
        at, count = end, count // 2
    return compose(maps[at + 1], maps[at])


def lanes_of(shape):
    return lax.broadcasted_iota(jnp.int32, shape, 1)


def packed(total, rows):
    n = total.shape[0]
    body, spare = 3 * n // 4, n // 4
    bottom = total[body:]
    side = jnp.concatenate(
        [pltpu.roll(bottom, (n - 32 * c) % LANES, 1) if 32 * c != n else bottom for c in range(3)],
        axis=0,
    )
    top = jnp.where(lanes_of(side.shape) < n, total[:body], side)
    offset = jnp.transpose(total)[n : n + 1]
    tail = jnp.concatenate([offset, rows, jnp.zeros((7 - rows.shape[0], n), f32)], axis=0)
    return top, jnp.pad(tail, ((0, 0), (0, LANES - n)))


def unpacked(lines, offset):
    body = lines.shape[0]
    spare = body // 3
    n = body + spare
    offset = jnp.broadcast_to(offset, (n, LANES))
    lane = lanes_of((spare, LANES))
    bottom = offset[body:]
    for c in range(3):
        part = pltpu.roll(lines[spare * c : spare * (c + 1)], (32 * c - n) % LANES, 1)
        bottom = jnp.where(lane // 32 == c, part, bottom)
    top = jnp.where(lanes_of(lines.shape) < n, lines, offset[:body])
    return jnp.concatenate([top, bottom], axis=0)


def summary_kernel(a_hbm, d_hbm, x_hbm, out_ref, maps, a_ref, d_ref, x_ref, sems):
    steps, n = d_ref.shape
    parts = 4
    size = steps // parts
    copies = [
        pltpu.make_async_copy(d_hbm, d_ref, sems.at[parts]),
        pltpu.make_async_copy(x_hbm, x_ref, sems.at[parts + 1]),
    ]
    blocks = []
    for c in range(parts):
        part = pl.ds(c * size, size)
        blocks.append(pltpu.make_async_copy(a_hbm.at[part], a_ref.at[part], sems.at[c]))
    for copy in copies[:1] + blocks + copies[1:]:
        copy.start()
    copies[0].wait()
    offsets = jnp.transpose(d_ref[...])
    for c in range(parts):
        blocks[c].wait()
        for t in range(c * size, (c + 1) * size):
            maps[t] = with_offset(a_ref[t], offsets[:, t : t + 1])
    total = rounds(maps, steps)
    copies[1].wait()
    top, tail = packed(total, x_ref[...])
    for j in range(out_ref.shape[0]):
        out_ref[j, : top.shape[0]] = top
        out_ref[j, top.shape[0] :] = tail


def prefix_kernel(k_ref, f_ref, maps, out_ref, rows_ref):
    steps, m, n = k_ref.shape
    feeds = jnp.transpose(f_ref[...])
    row, lane = (lax.broadcasted_iota(jnp.int32, (n, LANES), d) for d in (0, 1))
    unit = jnp.where(row == lane, 1.0, 0.0).astype(f32)

    def put(t, value):
        rows_ref[pl.ds(t, n, stride=steps)] = value

    def get(t):
        return rows_ref[pl.ds(t, n, stride=steps)]

    put(0, unit)
    size = steps
    while size > 1:
        size //= 2
        at = 2 * steps - 2 * (steps // size)
        put(size, maps[at])
        for t in range(2 * size, steps, 2 * size):
            put(t + size, compose(maps[at + t // size], get(t)))
    for t in range(steps):
        gain = with_offset(-k_ref[t], feeds[:, t : t + 1])
        rows_ref[pl.ds(n * steps + t, m, stride=steps)] = compose(gain, get(t))
    block = 512
    for at in range(0, (n + m) * steps, block):
        high, low = split(rows_ref[at : at + block])
        out_ref[at : at + block, :LANES] = high
        out_ref[at : at + block, LANES:] = low


def group_kernel(r_ref, out_ref, maps):
    count, lines, _ = r_ref.shape
    n = maps.shape[1]
    body = lines - 8
    heads = [
        jnp.concatenate([r_ref[j, body + k : body + k + 1] for j in range(count)], axis=0)
        for k in range(3)
    ]
    offsets = jnp.transpose(heads[0])[:n]
    for j in range(count):
        maps[j] = unpacked(r_ref[j, :body], offsets[:, j : j + 1])
    out_ref[:n] = rounds(maps, count)
    for s in range(2):
        out_ref[n + s * count : n + (s + 1) * count] = heads[1 + s]


def inner_kernel(i_ref, maps, out_ref):
    n = out_ref.shape[0]
    index = i_ref[0]
    row, lane = (lax.broadcasted_iota(jnp.int32, (n, LANES), d) for d in (0, 1))
    held = jnp.where(row == lane, 1.0, 0.0).astype(f32)
    held = jnp.where((index & 8) != 0, maps[28], held)
    for bit, first in ((4, 24), (2, 16), (1, 0)):
        at = first + (index // (2 * bit)) * 2
        held = jnp.where((index & bit) != 0, compose(maps[at], held), held)
    out_ref[...] = held


def apply_kernel(i_ref, own_ref, other_ref, inner_ref, maps_ref, out_ref):
    n = inner_ref.shape[0]
    second = i_ref[0] >= 16
    own, other = own_ref[n:], other_ref[n:]
    halves = jnp.where(second, other, own), jnp.where(second, own, other)
    start = jnp.concatenate([h[16 * s : 16 * s + 16] for s in (0, 1) for h in halves], axis=0)
    lane = lanes_of(start.shape)
    start = jnp.where(lane < n, start, jnp.where(lane == n, 1.0, 0.0))
    start = jnp.where(second, carry(start, other_ref[:n]), start)
    xh, xl = split(carry(start, inner_ref[...]))
    x = jnp.concatenate(
        [jnp.concatenate([xh, xh], axis=1), jnp.concatenate([xl, jnp.zeros_like(xl)], axis=1)],
        axis=0,
    )
    count = maps_ref.shape[0] // LANES
    first = count * 2 // 3
    rest = count - first
    for q in range(0, count, 2):
        value = dot_t(x, maps_ref[q * LANES : (q + 2) * LANES])
        value = value[:64] + value[64:]
        for p in (0, 1):
            for s in (0, 1):
                line = s * first + q + p if q < first else 2 * first + s * rest + q + p - first
                part = value[32 * s : 32 * s + 32, p * LANES : (p + 1) * LANES]
                out_ref[pl.ds(line, 32, stride=2 * count)] = part


def order_kernel(r_ref, states_hbm, controls_hbm, tile_ref, sems):
    lines = r_ref.shape[1]
    lane = lanes_of((lines, LANES)) // 32
    cut = states_hbm.shape[0]
    copies = []
    for g in range(8):
        parts = [r_ref[4 * g + b] for b in range(4)]
        for a in range(4):
            value = None
            for b in range(4):
                moved = parts[b] if a == b else pltpu.roll(parts[b], 32 * ((b - a) % 4), 1)
                value = moved if value is None else jnp.where(lane == b, moved, value)
            tile_ref[g, pl.ds(a, lines, stride=4)] = value
        across = pl.ds(g * LANES, LANES)
        for k, (rows, to) in enumerate(
            ((pl.ds(0, cut), states_hbm), (pl.ds(cut, 4 * lines - cut), controls_hbm))
        ):
            copies.append(
                pltpu.make_async_copy(tile_ref.at[g, rows], to.at[:, across], sems.at[2 * g + k])
            )
            copies[-1].start()
    for copy in copies:
        copy.wait()


VMEM = pl.BlockSpec(memory_space=pltpu.VMEM)
SMEM = pl.BlockSpec(memory_space=pltpu.SMEM)
HBM = pl.BlockSpec(memory_space=pltpu.HBM)


def call(kernel, outs, ins, to=VMEM, scratch=(), flops=0, limit=LIMIT):
    many = isinstance(outs, (list, tuple))
    return pl.pallas_call(
        kernel,
        out_shape=outs,
        in_specs=ins,
        out_specs=[to] * len(outs) if many else to,
        scratch_shapes=list(scratch),
        compiler_params=pltpu.CompilerParams(vmem_limit_bytes=limit),
        cost_estimate=pl.CostEstimate(flops=flops, bytes_accessed=4000000, transcendentals=0),
    )


def body(closed_loop, gains, feedforward, drift_terms, initial_states):
    steps, n, _ = closed_loop.shape
    m = gains.shape[1]
    blocks = lax.axis_size("tm")
    half = blocks // 2
    shape = jax.ShapeDtypeStruct
    index = lax.axis_index("tm").astype(jnp.int32)
    inner_index = (index % half).reshape(1)
    index = index.reshape(1)
    semaphores = pltpu.SemaphoreType.DMA

    payload, maps = call(
        summary_kernel,
        [shape((half, 3 * n // 4 + 8, LANES), f32), shape((2 * steps - 2, n, LANES), f32)],
        [HBM] * 3,
        scratch=[
            pltpu.VMEM((steps, n, n), f32),
            pltpu.VMEM((steps, n), f32),
            pltpu.VMEM((2, n), f32),
            semaphores((6,)),
        ],
        flops=300_000_000,
        limit=60 * 1024 * 1024,
    )(closed_loop, drift_terms, jnp.transpose(initial_states))
    groups = [[h * half + j for j in range(half)] for h in range(2)]
    gathered = lax.all_to_all(payload, "tm", 0, 0, tiled=True, axis_index_groups=groups)

    rows = (n + m) * steps
    local = call(
        prefix_kernel,
        shape((rows, 2 * LANES), bf16),
        [VMEM] * 3,
        scratch=[pltpu.VMEM((rows, LANES), f32)],
        flops=500_000_000,
    )(gains, feedforward, maps)
    gathered, local = lax.optimization_barrier((gathered, local))

    own, group_maps = call(
        group_kernel,
        [shape((n + 2 * half, LANES), f32), shape((2 * half - 2, n, LANES), f32)],
        [VMEM],
        flops=150_000_000,
    )(gathered)
    other = lax.ppermute(own, "tm", [(j, (j + half) % blocks) for j in range(blocks)])
    inner = call(inner_kernel, shape((n, LANES), f32), [SMEM, VMEM], flops=50_000_000)(
        inner_index, group_maps
    )

    lines = 2 * rows // LANES
    sent = call(
        apply_kernel,
        shape((blocks * lines, LANES), f32),
        [SMEM] + [VMEM] * 4,
        flops=300_000_000,
    )(index, own, other, inner, local)
    moved = lax.all_to_all(sent.reshape(blocks, lines, LANES), "tm", 0, 0, tiled=True)
    states, controls = call(
        order_kernel,
        [shape((2 * n, blocks * steps), f32), shape((2 * m, blocks * steps), f32)],
        [VMEM],
        to=HBM,
        scratch=[pltpu.VMEM((8, 4 * lines, LANES), f32), semaphores((16,))],
        flops=1_000_000,
    )(moved)
    return states.reshape(2, n, -1), controls.reshape(2, m, -1)


def solution(mesh):
    return jax.shard_map(
        body,
        mesh=mesh,
        in_specs=(
            P("tm", None, None),
            P("tm", None, None),
            P("tm", None),
            P("tm", None),
            P(None, ("tm", "scen")),
        ),
        out_specs=(P(("tm", "scen"), None, None), P(("tm", "scen"), None, None)),
        check_vma=False,
    )
```

```python
import jax
import jax.numpy as jnp
from jax import lax
from jax.experimental import pallas as pl
from jax.experimental.pallas import tpu as pltpu
from jax.sharding import PartitionSpec as P

f32, bf16 = jnp.float32, jnp.bfloat16
LANES = 128
LIMIT = 40 * 1024 * 1024


def split(x):
    high = x.astype(bf16)
    return high, (x - high.astype(f32)).astype(bf16)


def dot(a, b):
    return jnp.dot(a, b, preferred_element_type=f32)


def dot_t(a, b):
    return lax.dot_general(a, b, (((1,), (1,)), ((), ())), preferred_element_type=f32)


def extended(x):
    n = x.shape[0]
    high, low = split(x)
    shape = (LANES - n, LANES)
    row, lane = (lax.broadcasted_iota(jnp.int32, shape, d) for d in (0, 1))
    one = jnp.where((row == 0) & (lane >= n), 1.0, 0.0).astype(bf16)
    return (
        jnp.concatenate([high, one], axis=0),
        jnp.concatenate([low, jnp.zeros(shape, bf16)], axis=0),
    )


def compose(later, earlier):
    count = later.shape[0]
    both = dot(
        jnp.concatenate(split(later), axis=0), jnp.concatenate(extended(earlier), axis=1)
    )
    return both[:count, :LANES] + (both[:count, LANES:] + both[count:, :LANES])


def carry(rows, following):
    count = rows.shape[0]
    both = dot_t(
        jnp.concatenate(split(rows), axis=0), jnp.concatenate(extended(following), axis=0)
    )
    return both[:count, :LANES] + (both[:count, LANES:] + both[count:, :LANES])


def with_offset(matrix, offset):
    wide = jnp.broadcast_to(offset, (matrix.shape[0], LANES - matrix.shape[1]))
    return jnp.concatenate([matrix, wide], axis=1)


def rounds(maps, count, at=0):
    while count > 2:
        end = at + count
        for k in range(count // 2):
            maps[end + k] = compose(maps[at + 2 * k + 1], maps[at + 2 * k])
        at, count = end, count // 2
    return compose(maps[at + 1], maps[at])


def lanes_of(shape):
    return lax.broadcasted_iota(jnp.int32, shape, 1)


def packed(total, rows):
    n = total.shape[0]
    body, spare = 3 * n // 4, n // 4
    bottom = total[body:]
    side = jnp.concatenate(
        [pltpu.roll(bottom, (n - 32 * c) % LANES, 1) if 32 * c != n else bottom for c in range(3)],
        axis=0,
    )
    top = jnp.where(lanes_of(side.shape) < n, total[:body], side)
    offset = jnp.transpose(total)[n : n + 1]
    tail = jnp.concatenate([offset, rows, jnp.zeros((7 - rows.shape[0], n), f32)], axis=0)
    return top, jnp.pad(tail, ((0, 0), (0, LANES - n)))


def unpacked(lines, offset):
    body = lines.shape[0]
    spare = body // 3
    n = body + spare
    offset = jnp.broadcast_to(offset, (n, LANES))
    lane = lanes_of((spare, LANES))
    bottom = offset[body:]
    for c in range(3):
        part = pltpu.roll(lines[spare * c : spare * (c + 1)], (32 * c - n) % LANES, 1)
        bottom = jnp.where(lane // 32 == c, part, bottom)
    top = jnp.where(lanes_of(lines.shape) < n, lines, offset[:body])
    return jnp.concatenate([top, bottom], axis=0)


def summary_kernel(a_hbm, d_hbm, x_hbm, out_ref, a_ref, d_ref, x_ref, maps, sems):
    steps, n = d_ref.shape
    parts = 4
    size = steps // parts
    small = [
        pltpu.make_async_copy(d_hbm, d_ref, sems.at[parts]),
        pltpu.make_async_copy(x_hbm, x_ref, sems.at[parts + 1]),
    ]
    blocks = []
    for c in range(parts):
        part = pl.ds(c * size, size)
        blocks.append(pltpu.make_async_copy(a_hbm.at[part], a_ref.at[part], sems.at[c]))
    for copy in small[:1] + blocks + small[1:]:
        copy.start()
    small[0].wait()
    offsets = jnp.transpose(d_ref[...])
    for c in range(parts):
        blocks[c].wait()
        for t in range(c * size, (c + 1) * size, 2):
            pair = [with_offset(a_ref[k], offsets[:, k : k + 1]) for k in (t, t + 1)]
            maps[t // 2] = compose(pair[1], pair[0])
    total = rounds(maps, steps // 2)
    small[1].wait()
    top, tail = packed(total, x_ref[...])
    for j in range(out_ref.shape[0]):
        out_ref[j, : top.shape[0]] = top
        out_ref[j, top.shape[0] :] = tail


def prefix_kernel(a_ref, d_ref, k_ref, f_ref, out_ref, maps, rows_ref):
    steps, m, n = k_ref.shape
    feeds = jnp.transpose(f_ref[...])
    offsets = jnp.transpose(d_ref[...])
    for t in range(steps):
        maps[t] = with_offset(a_ref[t], offsets[:, t : t + 1])
    rounds(maps, steps)
    row, lane = (lax.broadcasted_iota(jnp.int32, (n, LANES), d) for d in (0, 1))
    unit = jnp.where(row == lane, 1.0, 0.0).astype(f32)

    def put(t, value):
        rows_ref[pl.ds(t, n, stride=steps)] = value

    def get(t):
        return rows_ref[pl.ds(t, n, stride=steps)]

    put(0, unit)
    size = steps
    while size > 1:
        size //= 2
        at = 2 * steps - 2 * (steps // size)
        put(size, maps[at])
        for t in range(2 * size, steps, 2 * size):
            put(t + size, compose(maps[at + t // size], get(t)))
    for t in range(steps):
        gain = with_offset(-k_ref[t], feeds[:, t : t + 1])
        rows_ref[pl.ds(n * steps + t, m, stride=steps)] = compose(gain, get(t))
    block = 512
    for at in range(0, (n + m) * steps, block):
        high, low = split(rows_ref[at : at + block])
        out_ref[at : at + block, :LANES] = high
        out_ref[at : at + block, LANES:] = low


def heads_of(r_ref, body):
    count = r_ref.shape[0]
    return [
        jnp.concatenate([r_ref[j, body + k : body + k + 1] for j in range(count)], axis=0)
        for k in range(3)
    ]


def unpack(r_ref, maps):
    count, lines, _ = r_ref.shape
    body = lines - 8
    heads = heads_of(r_ref, body)
    offsets = jnp.transpose(heads[0])[: maps.shape[1]]
    for j in range(count):
        maps[j] = unpacked(r_ref[j, :body], offsets[:, j : j + 1])
    return heads[1:]


def group_kernel(r_ref, out_ref, maps):
    count, n = r_ref.shape[0], maps.shape[1]
    starts = unpack(r_ref, maps)
    total = rounds(maps, count)
    for j in range(out_ref.shape[0]):
        out_ref[j, :n] = total
        for s in range(2):
            out_ref[j, n + s * count : n + (s + 1) * count] = starts[s]


def inner_kernel(i_ref, r_ref, out_ref, maps):
    n = out_ref.shape[0]
    index = i_ref[0]
    unpack(r_ref, maps)
    row, lane = (lax.broadcasted_iota(jnp.int32, (n, LANES), d) for d in (0, 1))
    held = jnp.where(row == lane, 1.0, 0.0).astype(f32)
    count = r_ref.shape[0]
    rounds(maps, count)
    bit = count // 2
    while bit:
        at = 2 * count - 2 * (count // bit) + (index // (2 * bit)) * 2
        held = jnp.where((index & bit) != 0, compose(maps[at], held), held)
        bit //= 2
    out_ref[...] = held


def apply_kernel(i_ref, rows_ref, inner_ref, maps_ref, out_ref):
    n = inner_ref.shape[0]
    row = i_ref[0]
    outer = rows_ref.shape[0]
    size = (rows_ref.shape[1] - n) // 2
    start = jnp.concatenate(
        [rows_ref[k, n + s * size : n + (s + 1) * size] for s in (0, 1) for k in range(outer)],
        axis=0,
    )
    lane = lanes_of(start.shape)
    start = jnp.where(lane < n, start, jnp.where(lane == n, 1.0, 0.0))
    for k in range(outer - 1):
        start = jnp.where(row > k, carry(start, rows_ref[k, :n]), start)
    xh, xl = split(carry(start, inner_ref[...]))
    x = jnp.concatenate(
        [jnp.concatenate([xh, xh], axis=1), jnp.concatenate([xl, jnp.zeros_like(xl)], axis=1)],
        axis=0,
    )
    count = maps_ref.shape[0] // LANES
    first = count * 2 // 3
    rest = count - first
    for q in range(0, count, 2):
        value = dot_t(x, maps_ref[q * LANES : (q + 2) * LANES])
        value = value[:64] + value[64:]
        for p in (0, 1):
            for s in (0, 1):
                line = s * first + q + p if q < first else 2 * first + s * rest + q + p - first
                part = value[32 * s : 32 * s + 32, p * LANES : (p + 1) * LANES]
                out_ref[pl.ds(line, 32, stride=2 * count)] = part


def order_kernel(r_ref, states_hbm, controls_hbm, tile_ref, sems):
    lines = r_ref.shape[1]
    lane = lanes_of((lines, LANES)) // 32
    cut = states_hbm.shape[0]
    copies = []
    for g in range(8):
        parts = [r_ref[4 * g + b] for b in range(4)]
        for a in range(4):
            value = None
            for b in range(4):
                moved = parts[b] if a == b else pltpu.roll(parts[b], 32 * ((b - a) % 4), 1)
                value = moved if value is None else jnp.where(lane == b, moved, value)
            tile_ref[g, pl.ds(a, lines, stride=4)] = value
        across = pl.ds(g * LANES, LANES)
        for k, (rows, to) in enumerate(
            ((pl.ds(0, cut), states_hbm), (pl.ds(cut, 4 * lines - cut), controls_hbm))
        ):
            copies.append(
                pltpu.make_async_copy(tile_ref.at[g, rows], to.at[:, across], sems.at[2 * g + k])
            )
            copies[-1].start()
    for copy in copies:
        copy.wait()


VMEM = pl.BlockSpec(memory_space=pltpu.VMEM)
SMEM = pl.BlockSpec(memory_space=pltpu.SMEM)
HBM = pl.BlockSpec(memory_space=pltpu.HBM)


def call(kernel, outs, ins, to=VMEM, scratch=(), flops=0, limit=LIMIT):
    many = isinstance(outs, (list, tuple))
    return pl.pallas_call(
        kernel,
        out_shape=outs,
        in_specs=ins,
        out_specs=[to] * len(outs) if many else to,
        scratch_shapes=list(scratch),
        compiler_params=pltpu.CompilerParams(vmem_limit_bytes=limit),
        cost_estimate=pl.CostEstimate(flops=flops, bytes_accessed=4000000, transcendentals=0),
    )


def body(closed_loop, gains, feedforward, drift_terms, initial_states):
    steps, n, _ = closed_loop.shape
    m = gains.shape[1]
    blocks = lax.axis_size("tm")
    inner, outer = 8, blocks // 8
    shape = jax.ShapeDtypeStruct
    index = lax.axis_index("tm").astype(jnp.int32)
    at_inner, at_outer = (index % inner).reshape(1), (index // inner).reshape(1)
    near = [[k * inner + j for j in range(inner)] for k in range(outer)]
    far = [[k * inner + j for k in range(outer)] for j in range(inner)]
    semaphores = pltpu.SemaphoreType.DMA

    payload = call(
        summary_kernel,
        shape((inner, 3 * n // 4 + 8, LANES), f32),
        [HBM] * 3,
        scratch=[
            pltpu.VMEM((steps, n, n), f32),
            pltpu.VMEM((steps, n), f32),
            pltpu.VMEM((2, n), f32),
            pltpu.VMEM((steps, n, LANES), f32),
            semaphores((6,)),
        ],
        flops=300_000_000,
        limit=60 * 1024 * 1024,
    )(closed_loop, drift_terms, jnp.transpose(initial_states))
    gathered = lax.all_to_all(payload, "tm", 0, 0, tiled=True, axis_index_groups=near)

    rows = (n + m) * steps
    local = call(
        prefix_kernel,
        shape((rows, 2 * LANES), bf16),
        [VMEM] * 4,
        scratch=[
            pltpu.VMEM((2 * steps, n, LANES), f32),
            pltpu.VMEM((rows, LANES), f32),
        ],
        flops=500_000_000,
    )(closed_loop, drift_terms, gains, feedforward)
    gathered, local = lax.optimization_barrier((gathered, local))

    group = call(
        group_kernel,
        shape((outer, n + 2 * inner, LANES), f32),
        [VMEM],
        scratch=[pltpu.VMEM((2 * inner, n, LANES), f32)],
        flops=150_000_000,
    )(gathered)
    across = lax.all_to_all(group, "tm", 0, 0, tiled=True, axis_index_groups=far)
    before = call(
        inner_kernel,
        shape((n, LANES), f32),
        [SMEM, VMEM],
        scratch=[pltpu.VMEM((2 * inner, n, LANES), f32)],
        flops=150_000_000,
    )(at_inner, gathered)
    across, before = lax.optimization_barrier((across, before))

    lines = 2 * rows // LANES
    sent = call(
        apply_kernel,
        shape((blocks * lines, LANES), f32),
        [SMEM] + [VMEM] * 3,
        flops=300_000_000,
    )(at_outer, across, before, local)
    moved = lax.all_to_all(sent.reshape(blocks, lines, LANES), "tm", 0, 0, tiled=True)
    states, controls = call(
        order_kernel,
        [shape((2 * n, blocks * steps), f32), shape((2 * m, blocks * steps), f32)],
        [VMEM],
        to=HBM,
        scratch=[pltpu.VMEM((8, 4 * lines, LANES), f32), semaphores((16,))],
        flops=1_000_000,
    )(moved)
    return states.reshape(2, n, -1), controls.reshape(2, m, -1)


def solution(mesh):
    return jax.shard_map(
        body,
        mesh=mesh,
        in_specs=(
            P("tm", None, None),
            P("tm", None, None),
            P("tm", None),
            P("tm", None),
            P(None, ("tm", "scen")),
        ),
        out_specs=(P(("tm", "scen"), None, None), P(("tm", "scen"), None, None)),
        check_vma=False,
    )
```

```python
import jax
import jax.numpy as jnp
from jax import lax
from jax.experimental import pallas as pl
from jax.experimental.pallas import tpu as pltpu
from jax.sharding import PartitionSpec as P

f32, bf16 = jnp.float32, jnp.bfloat16
LANES = 128
LIMIT = 40 * 1024 * 1024


def split(x):
    high = x.astype(bf16)
    return high, (x - high.astype(f32)).astype(bf16)


def dot(a, b):
    return jnp.dot(a, b, preferred_element_type=f32)


def dot_t(a, b):
    return lax.dot_general(a, b, (((1,), (1,)), ((), ())), preferred_element_type=f32)


def extended(x, lane_of=0):
    n = x.shape[0]
    high, low = split(x)
    shape = (LANES - n, LANES)
    row, lane = (lax.broadcasted_iota(jnp.int32, shape, d) for d in (0, 1))
    one = jnp.where((row == lane_of) & (lane >= n), 1.0, 0.0).astype(bf16)
    return (
        jnp.concatenate([high, one], axis=0),
        jnp.concatenate([low, jnp.zeros(shape, bf16)], axis=0),
    )


def compose(later, earlier, lane_of=0):
    count = later.shape[0]
    both = dot(
        jnp.concatenate(split(later), axis=0), jnp.concatenate(extended(earlier, lane_of), axis=1)
    )
    return both[:count, :LANES] + (both[:count, LANES:] + both[count:, :LANES])


def carry(rows, following):
    count = rows.shape[0]
    both = dot_t(
        jnp.concatenate(split(rows), axis=0), jnp.concatenate(extended(following), axis=0)
    )
    return both[:count, :LANES] + (both[:count, LANES:] + both[count:, :LANES])


def columns(rows, n):
    count, width = rows.shape
    if width < n:
        rows = jnp.pad(rows, ((0, 0), (0, n - width)))
    turned = jnp.transpose(rows)
    if count < LANES - n:
        turned = jnp.pad(turned, ((0, 0), (0, LANES - n - count)))
    return turned


def with_offsets(matrix, offsets):
    return jnp.concatenate([matrix, offsets[: matrix.shape[0]]], axis=1)


def rounds(maps, count, size=1):
    at = 0
    while count > 2:
        end = at + count
        for k in range(count // 2):
            maps[end + k] = compose(maps[at + 2 * k + 1], maps[at + 2 * k], (2 * k + 1) * size)
        at, count, size = end, count // 2, 2 * size
    return compose(maps[at + 1], maps[at], size)


def lanes_of(shape):
    return lax.broadcasted_iota(jnp.int32, shape, 1)


def packed(total, rows):
    n = total.shape[0]
    body, spare = 3 * n // 4, n // 4
    bottom = total[body:]
    side = jnp.concatenate(
        [pltpu.roll(bottom, (n - 32 * c) % LANES, 1) if 32 * c != n else bottom for c in range(3)],
        axis=0,
    )
    top = jnp.where(lanes_of(side.shape) < n, total[:body], side)
    offset = jnp.transpose(total)[n : n + 1]
    tail = jnp.concatenate([offset, rows, jnp.zeros((7 - rows.shape[0], n), f32)], axis=0)
    return top, jnp.pad(tail, ((0, 0), (0, LANES - n)))


def unpacked(lines, offset):
    body = lines.shape[0]
    spare = body // 3
    n = body + spare
    lane = lanes_of((spare, LANES))
    bottom = offset[body:]
    for c in range(3):
        part = pltpu.roll(lines[spare * c : spare * (c + 1)], (32 * c - n) % LANES, 1)
        bottom = jnp.where(lane // 32 == c, part, bottom)
    top = jnp.where(lanes_of(lines.shape) < n, lines, offset[:body])
    return jnp.concatenate([top, bottom], axis=0)


def summary_kernel(a_hbm, d_hbm, x_hbm, out_ref, a_ref, d_ref, x_ref, maps, sems):
    steps, n = d_ref.shape
    parts = 2
    size = steps // parts
    small = [
        pltpu.make_async_copy(d_hbm, d_ref, sems.at[parts]),
        pltpu.make_async_copy(x_hbm, x_ref, sems.at[parts + 1]),
    ]
    blocks = []
    for c in range(parts):
        part = pl.ds(c * size, size)
        blocks.append(pltpu.make_async_copy(a_hbm.at[part], a_ref.at[part], sems.at[c]))
    for copy in small[:1] + blocks + small[1:]:
        copy.start()
    small[0].wait()
    offsets = columns(d_ref[...], n)
    for c in range(parts):
        blocks[c].wait()
        for t in range(c * size, (c + 1) * size, 2):
            pair = [with_offsets(a_ref[k], offsets) for k in (t, t + 1)]
            maps[t // 2] = compose(pair[1], pair[0], t + 1)
    total = rounds(maps, steps // 2, 2)
    small[1].wait()
    top, tail = packed(total, x_ref[...])
    for j in range(out_ref.shape[0]):
        out_ref[j, : top.shape[0]] = top
        out_ref[j, top.shape[0] :] = tail


def prefix_kernel(a_ref, d_ref, k_ref, f_ref, out_ref, maps, rows_ref):
    steps, m, n = k_ref.shape
    feeds = columns(f_ref[...], n)
    offsets = columns(d_ref[...], n)
    for t in range(steps):
        maps[t] = with_offsets(a_ref[t], offsets)
    rounds(maps, steps)
    row, lane = (lax.broadcasted_iota(jnp.int32, (n, LANES), d) for d in (0, 1))
    unit = jnp.where(row == lane, 1.0, 0.0).astype(f32)

    def put(t, value):
        rows_ref[pl.ds(t, n, stride=steps)] = value

    def get(t):
        return rows_ref[pl.ds(t, n, stride=steps)]

    put(0, unit)
    size = steps
    while size > 1:
        size //= 2
        at = 2 * steps - 2 * (steps // size)
        put(size, maps[at])
        for t in range(2 * size, steps, 2 * size):
            put(t + size, compose(maps[at + t // size], get(t), t))
    for t in range(steps):
        gain = with_offsets(-k_ref[t], feeds)
        rows_ref[pl.ds(n * steps + t, m, stride=steps)] = compose(gain, get(t), t)
    block = 512
    for at in range(0, (n + m) * steps, block):
        high, low = split(rows_ref[at : at + block])
        out_ref[at : at + block, :LANES] = high
        out_ref[at : at + block, LANES:] = low


def heads_of(r_ref, body):
    count = r_ref.shape[0]
    return [
        jnp.concatenate([r_ref[j, body + k : body + k + 1] for j in range(count)], axis=0)
        for k in range(3)
    ]


def unpack(r_ref, maps):
    count, lines, _ = r_ref.shape
    n = maps.shape[1]
    body = lines - 8
    heads = heads_of(r_ref, body)
    offsets = with_offsets(jnp.zeros((n, n), f32), columns(heads[0][:, :n], n))
    for j in range(count):
        maps[j] = unpacked(r_ref[j, :body], offsets)
    return heads[1:]


def group_kernel(r_ref, out_ref, maps):
    count, n = r_ref.shape[0], maps.shape[1]
    starts = unpack(r_ref, maps)
    total = rounds(maps, count)
    for j in range(out_ref.shape[0]):
        out_ref[j, :n] = total
        for s in range(2):
            out_ref[j, n + s * count : n + (s + 1) * count] = starts[s]


def inner_kernel(i_ref, r_ref, out_ref, maps):
    n = out_ref.shape[0]
    index = i_ref[0]
    unpack(r_ref, maps)
    row, lane = (lax.broadcasted_iota(jnp.int32, (n, LANES), d) for d in (0, 1))
    held = jnp.where(row == lane, 1.0, 0.0).astype(f32)
    count = r_ref.shape[0]
    rounds(maps, count)
    bit = count // 2
    while bit:
        pair = index // (2 * bit)
        at = 2 * count - 2 * (count // bit) + pair * 2
        held = jnp.where((index & bit) != 0, compose(maps[at], held, pair * 2 * bit), held)
        bit //= 2
    out_ref[...] = held


def apply_kernel(i_ref, rows_ref, inner_ref, maps_ref, out_ref):
    n = inner_ref.shape[0]
    row = i_ref[0]
    outer = rows_ref.shape[0]
    size = (rows_ref.shape[1] - n) // 2
    start = jnp.concatenate(
        [rows_ref[k, n + s * size : n + (s + 1) * size] for s in (0, 1) for k in range(outer)],
        axis=0,
    )
    lane = lanes_of(start.shape)
    start = jnp.where(lane < n, start, jnp.where(lane == n, 1.0, 0.0))
    first = jnp.where(row > 1, compose(rows_ref[1, :n], rows_ref[0, :n]), rows_ref[0, :n])
    second = jnp.where(row > 2, compose(inner_ref[...], rows_ref[2, :n]), inner_ref[...])
    start = jnp.where(row > 0, carry(start, first), start)
    xh, xl = split(carry(start, second))
    x = jnp.concatenate(
        [jnp.concatenate([xh, xh], axis=1), jnp.concatenate([xl, jnp.zeros_like(xl)], axis=1)],
        axis=0,
    )
    count = maps_ref.shape[0] // LANES
    first = count * 2 // 3
    rest = count - first
    for q in range(0, count, 2):
        value = dot_t(x, maps_ref[q * LANES : (q + 2) * LANES])
        value = value[:64] + value[64:]
        for p in (0, 1):
            for s in (0, 1):
                line = s * first + q + p if q < first else 2 * first + s * rest + q + p - first
                part = value[32 * s : 32 * s + 32, p * LANES : (p + 1) * LANES]
                out_ref[pl.ds(line, 32, stride=2 * count)] = part


def order_kernel(r_ref, states_hbm, controls_hbm, tile_ref, sems):
    lines = r_ref.shape[1]
    lane = lanes_of((lines, LANES)) // 32
    cut = states_hbm.shape[0]
    copies = []
    for g in range(8):
        parts = [r_ref[4 * g + b] for b in range(4)]
        for a in range(4):
            value = None
            for b in range(4):
                moved = parts[b] if a == b else pltpu.roll(parts[b], 32 * ((b - a) % 4), 1)
                value = moved if value is None else jnp.where(lane == b, moved, value)
            tile_ref[g, pl.ds(a, lines, stride=4)] = value
        across = pl.ds(g * LANES, LANES)
        for k, (rows, to) in enumerate(
            ((pl.ds(0, cut), states_hbm), (pl.ds(cut, 4 * lines - cut), controls_hbm))
        ):
            copies.append(
                pltpu.make_async_copy(tile_ref.at[g, rows], to.at[:, across], sems.at[2 * g + k])
            )
            copies[-1].start()
    for copy in copies:
        copy.wait()


VMEM = pl.BlockSpec(memory_space=pltpu.VMEM)
SMEM = pl.BlockSpec(memory_space=pltpu.SMEM)
HBM = pl.BlockSpec(memory_space=pltpu.HBM)


def call(kernel, outs, ins, to=VMEM, scratch=(), flops=0, limit=LIMIT):
    many = isinstance(outs, (list, tuple))
    return pl.pallas_call(
        kernel,
        out_shape=outs,
        in_specs=ins,
        out_specs=[to] * len(outs) if many else to,
        scratch_shapes=list(scratch),
        compiler_params=pltpu.CompilerParams(vmem_limit_bytes=limit),
        cost_estimate=pl.CostEstimate(flops=flops, bytes_accessed=4000000, transcendentals=0),
    )


def body(closed_loop, gains, feedforward, drift_terms, initial_states):
    steps, n, _ = closed_loop.shape
    m = gains.shape[1]
    blocks = lax.axis_size("tm")
    inner, outer = 8, blocks // 8
    shape = jax.ShapeDtypeStruct
    index = lax.axis_index("tm").astype(jnp.int32)
    at_inner, at_outer = (index % inner).reshape(1), (index // inner).reshape(1)
    near = [[k * inner + j for j in range(inner)] for k in range(outer)]
    far = [[k * inner + j for k in range(outer)] for j in range(inner)]
    semaphores = pltpu.SemaphoreType.DMA

    payload = call(
        summary_kernel,
        shape((inner, 3 * n // 4 + 8, LANES), f32),
        [HBM] * 3,
        scratch=[
            pltpu.VMEM((steps, n, n), f32),
            pltpu.VMEM((steps, n), f32),
            pltpu.VMEM((2, n), f32),
            pltpu.VMEM((steps, n, LANES), f32),
            semaphores((6,)),
        ],
        flops=300_000_000,
        limit=60 * 1024 * 1024,
    )(closed_loop, drift_terms, jnp.transpose(initial_states))
    gathered = lax.all_to_all(payload, "tm", 0, 0, tiled=True, axis_index_groups=near)

    rows = (n + m) * steps
    local = call(
        prefix_kernel,
        shape((rows, 2 * LANES), bf16),
        [VMEM] * 4,
        scratch=[
            pltpu.VMEM((2 * steps, n, LANES), f32),
            pltpu.VMEM((rows, LANES), f32),
        ],
        flops=500_000_000,
    )(closed_loop, drift_terms, gains, feedforward)
    gathered, local = lax.optimization_barrier((gathered, local))

    group = call(
        group_kernel,
        shape((outer, n + 2 * inner, LANES), f32),
        [VMEM],
        scratch=[pltpu.VMEM((2 * inner, n, LANES), f32)],
        flops=150_000_000,
    )(gathered)
    across = lax.all_to_all(group, "tm", 0, 0, tiled=True, axis_index_groups=far)
    before = call(
        inner_kernel,
        shape((n, LANES), f32),
        [SMEM, VMEM],
        scratch=[pltpu.VMEM((2 * inner, n, LANES), f32)],
        flops=150_000_000,
    )(at_inner, gathered)
    across, before = lax.optimization_barrier((across, before))

    lines = 2 * rows // LANES
    sent = call(
        apply_kernel,
        shape((blocks * lines, LANES), f32),
        [SMEM] + [VMEM] * 3,
        flops=300_000_000,
    )(at_outer, across, before, local)
    moved = lax.all_to_all(sent.reshape(blocks, lines, LANES), "tm", 0, 0, tiled=True)
    states, controls = call(
        order_kernel,
        [shape((2 * n, blocks * steps), f32), shape((2 * m, blocks * steps), f32)],
        [VMEM],
        to=HBM,
        scratch=[pltpu.VMEM((8, 4 * lines, LANES), f32), semaphores((16,))],
        flops=1_000_000,
    )(moved)
    return states.reshape(2, n, -1), controls.reshape(2, m, -1)


def solution(mesh):
    return jax.shard_map(
        body,
        mesh=mesh,
        in_specs=(
            P("tm", None, None),
            P("tm", None, None),
            P("tm", None),
            P("tm", None),
            P(None, ("tm", "scen")),
        ),
        out_specs=(P(("tm", "scen"), None, None), P(("tm", "scen"), None, None)),
        check_vma=False,
    )
```

```python
import jax
import jax.numpy as jnp
from jax import lax
from jax.experimental import pallas as pl
from jax.experimental.pallas import tpu as pltpu
from jax.sharding import PartitionSpec as P

f32, bf16 = jnp.float32, jnp.bfloat16
LANES = 128
LIMIT = 40 * 1024 * 1024


def split(x):
    high = x.astype(bf16)
    return high, (x - high.astype(f32)).astype(bf16)


def dot(a, b):
    return jnp.dot(a, b, preferred_element_type=f32)


def dot_t(a, b):
    return lax.dot_general(a, b, (((1,), (1,)), ((), ())), preferred_element_type=f32)


def extended(x, lane_of=0):
    n = x.shape[0]
    high, low = split(x)
    shape = (LANES - n, LANES)
    row, lane = (lax.broadcasted_iota(jnp.int32, shape, d) for d in (0, 1))
    one = jnp.where((row == lane_of) & (lane >= n), 1.0, 0.0).astype(bf16)
    return (
        jnp.concatenate([high, one], axis=0),
        jnp.concatenate([low, jnp.zeros(shape, bf16)], axis=0),
    )


def compose(later, earlier, lane_of=0):
    count = later.shape[0]
    both = dot(
        jnp.concatenate(split(later), axis=0), jnp.concatenate(extended(earlier, lane_of), axis=1)
    )
    return both[:count, :LANES] + (both[:count, LANES:] + both[count:, :LANES])


def carry(rows, following):
    count = rows.shape[0]
    both = dot_t(
        jnp.concatenate(split(rows), axis=0), jnp.concatenate(extended(following), axis=0)
    )
    return both[:count, :LANES] + (both[:count, LANES:] + both[count:, :LANES])


def columns(rows, n):
    count, width = rows.shape
    if width < n:
        rows = jnp.pad(rows, ((0, 0), (0, n - width)))
    turned = jnp.transpose(rows)
    if count < LANES - n:
        turned = jnp.pad(turned, ((0, 0), (0, LANES - n - count)))
    return turned


def with_offsets(matrix, offsets):
    return jnp.concatenate([matrix, offsets[: matrix.shape[0]]], axis=1)


def rounds(maps, count, size=1):
    at = 0
    while count > 2:
        end = at + count
        for k in range(count // 2):
            maps[end + k] = compose(maps[at + 2 * k + 1], maps[at + 2 * k], (2 * k + 1) * size)
        at, count, size = end, count // 2, 2 * size
    return compose(maps[at + 1], maps[at], size)


def lanes_of(shape):
    return lax.broadcasted_iota(jnp.int32, shape, 1)


def packed(total, rows):
    n = total.shape[0]
    body, spare = 3 * n // 4, n // 4
    bottom = total[body:]
    side = jnp.concatenate(
        [pltpu.roll(bottom, (n - 32 * c) % LANES, 1) if 32 * c != n else bottom for c in range(3)],
        axis=0,
    )
    top = jnp.where(lanes_of(side.shape) < n, total[:body], side)
    offset = jnp.transpose(total)[n : n + 1]
    tail = jnp.concatenate([offset, rows, jnp.zeros((7 - rows.shape[0], n), f32)], axis=0)
    return top, jnp.pad(tail, ((0, 0), (0, LANES - n)))


def unpacked(lines, offset):
    body = lines.shape[0]
    spare = body // 3
    n = body + spare
    lane = lanes_of((spare, LANES))
    bottom = offset[body:]
    for c in range(3):
        part = pltpu.roll(lines[spare * c : spare * (c + 1)], (32 * c - n) % LANES, 1)
        bottom = jnp.where(lane // 32 == c, part, bottom)
    top = jnp.where(lanes_of(lines.shape) < n, lines, offset[:body])
    return jnp.concatenate([top, bottom], axis=0)


def summary_kernel(a_hbm, d_hbm, x_hbm, out_ref, a_ref, d_ref, x_ref, maps, sems):
    steps, n = d_ref.shape
    parts = 2
    size = steps // parts
    small = [
        pltpu.make_async_copy(d_hbm, d_ref, sems.at[parts]),
        pltpu.make_async_copy(x_hbm, x_ref, sems.at[parts + 1]),
    ]
    blocks = []
    for c in range(parts):
        part = pl.ds(c * size, size)
        blocks.append(pltpu.make_async_copy(a_hbm.at[part], a_ref.at[part], sems.at[c]))
    for copy in small[:1] + blocks + small[1:]:
        copy.start()
    small[0].wait()
    offsets = columns(d_ref[...], n)
    for c in range(parts):
        blocks[c].wait()
        for t in range(c * size, (c + 1) * size, 2):
            pair = [with_offsets(a_ref[k], offsets) for k in (t, t + 1)]
            maps[t // 2] = compose(pair[1], pair[0], t + 1)
    total = rounds(maps, steps // 2, 2)
    small[1].wait()
    top, tail = packed(total, x_ref[...])
    for j in range(out_ref.shape[0]):
        out_ref[j, : top.shape[0]] = top
        out_ref[j, top.shape[0] :] = tail


def prefix_kernel(i_ref, a_ref, d_ref, k_ref, f_ref, out_ref, maps, rows_ref):
    steps, m, n = k_ref.shape
    feeds = columns(f_ref[...], n)
    offsets = columns(d_ref[...], n)
    for t in range(steps):
        maps[t] = with_offsets(a_ref[t], offsets)
    rounds(maps, steps)
    row, lane = (lax.broadcasted_iota(jnp.int32, (n, LANES), d) for d in (0, 1))
    unit = jnp.where(row == lane, 1.0, 0.0).astype(f32)

    def put(t, value):
        rows_ref[pl.ds(t, n, stride=steps)] = value

    def get(t):
        return rows_ref[pl.ds(t, n, stride=steps)]

    put(0, unit)
    size = steps
    while size > 1:
        size //= 2
        at = 2 * steps - 2 * (steps // size)
        put(size, maps[at])
        for t in range(2 * size, steps, 2 * size):
            put(t + size, compose(maps[at + t // size], get(t), t))
    for t in range(steps):
        gain = with_offsets(-k_ref[t], feeds)
        rows_ref[pl.ds(n * steps + t, m, stride=steps)] = compose(gain, get(t), t)
    turned = [pl.multiple_of((i_ref[0] + k) % 4 * steps, steps) for k in range(4)]
    for at in range(0, (n + m) * steps, LANES):
        high, low = split(rows_ref[at : at + LANES])
        for k in range(4):
            part = slice(k * steps, (k + 1) * steps)
            out_ref[pl.ds(at + turned[k], steps), :LANES] = high[part]
            out_ref[pl.ds(at + turned[k], steps), LANES:] = low[part]


def heads_of(r_ref, body):
    count = r_ref.shape[0]
    return [
        jnp.concatenate([r_ref[j, body + k : body + k + 1] for j in range(count)], axis=0)
        for k in range(3)
    ]


def unpack(r_ref, maps):
    count, lines, _ = r_ref.shape
    n = maps.shape[1]
    body = lines - 8
    heads = heads_of(r_ref, body)
    offsets = with_offsets(jnp.zeros((n, n), f32), columns(heads[0][:, :n], n))
    for j in range(count):
        maps[j] = unpacked(r_ref[j, :body], offsets)
    return heads[1:]


def group_kernel(i_ref, r_ref, out_ref, inner_ref, maps):
    count, n = r_ref.shape[0], maps.shape[1]
    index = i_ref[0]
    starts = unpack(r_ref, maps)
    total = rounds(maps, count)
    row, lane = (lax.broadcasted_iota(jnp.int32, (n, LANES), d) for d in (0, 1))
    held = jnp.where(row == lane, 1.0, 0.0).astype(f32)
    bit = count // 2
    while bit:
        pair = index // (2 * bit)
        at = 2 * count - 2 * (count // bit) + pair * 2
        held = jnp.where((index & bit) != 0, compose(maps[at], held, pair * 2 * bit), held)
        bit //= 2
    inner_ref[...] = held
    for j in range(out_ref.shape[0]):
        out_ref[j, :n] = total
        for s in range(2):
            out_ref[j, n + s * count : n + (s + 1) * count] = starts[s]


def apply_kernel(i_ref, rows_ref, inner_ref, maps_ref, out_ref):
    n = inner_ref.shape[0]
    row = i_ref[0]
    outer = rows_ref.shape[0]
    size = (rows_ref.shape[1] - n) // 2
    start = jnp.concatenate(
        [rows_ref[k, n + s * size : n + (s + 1) * size] for s in (0, 1) for k in range(outer)],
        axis=0,
    )
    lane = lanes_of(start.shape)
    start = jnp.where(lane < n, start, jnp.where(lane == n, 1.0, 0.0))
    first = jnp.where(row > 1, compose(rows_ref[1, :n], rows_ref[0, :n]), rows_ref[0, :n])
    second = jnp.where(row > 2, compose(inner_ref[...], rows_ref[2, :n]), inner_ref[...])
    start = jnp.where(row > 0, carry(start, first), start)
    xh, xl = split(carry(start, second))
    x = jnp.concatenate(
        [jnp.concatenate([xh, xh], axis=1), jnp.concatenate([xl, jnp.zeros_like(xl)], axis=1)],
        axis=0,
    )
    count = maps_ref.shape[0] // LANES
    first = count * 2 // 3
    rest = count - first
    for q in range(0, count, 2):
        value = dot_t(x, maps_ref[q * LANES : (q + 2) * LANES])
        value = value[:64] + value[64:]
        for p in (0, 1):
            for s in (0, 1):
                line = s * first + q + p if q < first else 2 * first + s * rest + q + p - first
                part = value[32 * s : 32 * s + 32, p * LANES : (p + 1) * LANES]
                out_ref[pl.ds(line, 32, stride=2 * count)] = part


def order_kernel(r_ref, states_hbm, controls_hbm, tile_ref, sems):
    lines = r_ref.shape[1]
    lane = lanes_of((lines, LANES)) // 32
    cut = states_hbm.shape[0]
    copies = []
    for g in range(8):
        parts = [r_ref[4 * g + b] for b in range(4)]
        for a in range(4):
            value = parts[0]
            for b in range(1, 4):
                value = jnp.where(lane == (a + b) % 4, parts[b], value)
            if a:
                value = pltpu.roll(value, LANES - 32 * a, 1)
            tile_ref[g, pl.ds(a, lines, stride=4)] = value
        across = pl.ds(g * LANES, LANES)
        for k, (rows, to) in enumerate(
            ((pl.ds(0, cut), states_hbm), (pl.ds(cut, 4 * lines - cut), controls_hbm))
        ):
            copies.append(
                pltpu.make_async_copy(tile_ref.at[g, rows], to.at[:, across], sems.at[2 * g + k])
            )
            copies[-1].start()
    for copy in copies:
        copy.wait()


VMEM = pl.BlockSpec(memory_space=pltpu.VMEM)
SMEM = pl.BlockSpec(memory_space=pltpu.SMEM)
HBM = pl.BlockSpec(memory_space=pltpu.HBM)


def call(kernel, outs, ins, to=VMEM, scratch=(), flops=0, limit=LIMIT):
    many = isinstance(outs, (list, tuple))
    return pl.pallas_call(
        kernel,
        out_shape=outs,
        in_specs=ins,
        out_specs=[to] * len(outs) if many else to,
        scratch_shapes=list(scratch),
        compiler_params=pltpu.CompilerParams(vmem_limit_bytes=limit),
        cost_estimate=pl.CostEstimate(flops=flops, bytes_accessed=4000000, transcendentals=0),
    )


def body(closed_loop, gains, feedforward, drift_terms, initial_states):
    steps, n, _ = closed_loop.shape
    m = gains.shape[1]
    blocks = lax.axis_size("tm")
    inner, outer = 8, blocks // 8
    shape = jax.ShapeDtypeStruct
    index = lax.axis_index("tm").astype(jnp.int32).reshape(1)
    at_inner, at_outer = index % inner, index // inner
    near = [[k * inner + j for j in range(inner)] for k in range(outer)]
    far = [[k * inner + j for k in range(outer)] for j in range(inner)]
    semaphores = pltpu.SemaphoreType.DMA

    payload = call(
        summary_kernel,
        shape((inner, 3 * n // 4 + 8, LANES), f32),
        [HBM] * 3,
        scratch=[
            pltpu.VMEM((steps, n, n), f32),
            pltpu.VMEM((steps, n), f32),
            pltpu.VMEM((2, n), f32),
            pltpu.VMEM((steps, n, LANES), f32),
            semaphores((6,)),
        ],
        flops=300_000_000,
        limit=60 * 1024 * 1024,
    )(closed_loop, drift_terms, jnp.transpose(initial_states))
    gathered = lax.all_to_all(payload, "tm", 0, 0, tiled=True, axis_index_groups=near)

    rows = (n + m) * steps
    local = call(
        prefix_kernel,
        shape((rows, 2 * LANES), bf16),
        [SMEM] + [VMEM] * 4,
        scratch=[
            pltpu.VMEM((2 * steps, n, LANES), f32),
            pltpu.VMEM((rows, LANES), f32),
        ],
        flops=500_000_000,
    )(index, closed_loop, drift_terms, gains, feedforward)
    gathered, local, at_inner, at_outer = lax.optimization_barrier(
        (gathered, local, at_inner, at_outer)
    )

    group, before = call(
        group_kernel,
        [shape((outer, n + 2 * inner, LANES), f32), shape((n, LANES), f32)],
        [SMEM, VMEM],
        scratch=[pltpu.VMEM((2 * inner, n, LANES), f32)],
        flops=150_000_000,
    )(at_inner, gathered)
    across = lax.all_to_all(group, "tm", 0, 0, tiled=True, axis_index_groups=far)

    lines = 2 * rows // LANES
    sent = call(
        apply_kernel,
        shape((blocks * lines, LANES), f32),
        [SMEM] + [VMEM] * 3,
        flops=300_000_000,
    )(at_outer, across, before, local)
    moved = lax.all_to_all(sent.reshape(blocks, lines, LANES), "tm", 0, 0, tiled=True)
    states, controls = call(
        order_kernel,
        [shape((2 * n, blocks * steps), f32), shape((2 * m, blocks * steps), f32)],
        [VMEM],
        to=HBM,
        scratch=[pltpu.VMEM((8, 4 * lines, LANES), f32), semaphores((16,))],
        flops=1_000_000,
    )(moved)
    return states.reshape(2, n, -1), controls.reshape(2, m, -1)


def solution(mesh):
    return jax.shard_map(
        body,
        mesh=mesh,
        in_specs=(
            P("tm", None, None),
            P("tm", None, None),
            P("tm", None),
            P("tm", None),
            P(None, ("tm", "scen")),
        ),
        out_specs=(P(("tm", "scen"), None, None), P(("tm", "scen"), None, None)),
        check_vma=False,
    )
```

```python
import jax
import jax.numpy as jnp
from jax import lax
from jax.experimental import pallas as pl
from jax.experimental.pallas import tpu as pltpu
from jax.sharding import PartitionSpec as P

f32, bf16 = jnp.float32, jnp.bfloat16
LANES = 128
LIMIT = 40 * 1024 * 1024

ALONG, ACROSS = (0, 4, 2, 6, 1, 5, 3, 7), (0, 2, 1, 3)


def split(x):
    high = x.astype(bf16)
    return high, (x - high.astype(f32)).astype(bf16)


def dot(a, b):
    return jnp.dot(a, b, preferred_element_type=f32)


def dot_t(a, b):
    return lax.dot_general(a, b, (((1,), (1,)), ((), ())), preferred_element_type=f32)


def extended(x, lane_of=0):
    n = x.shape[0]
    high, low = split(x)
    shape = (LANES - n, LANES)
    row, lane = (lax.broadcasted_iota(jnp.int32, shape, d) for d in (0, 1))
    one = jnp.where((row == lane_of) & (lane >= n), 1.0, 0.0).astype(bf16)
    return (
        jnp.concatenate([high, one], axis=0),
        jnp.concatenate([low, jnp.zeros(shape, bf16)], axis=0),
    )


def compose(later, earlier, lane_of=0):
    count = later.shape[0]
    both = dot(
        jnp.concatenate(split(later), axis=0), jnp.concatenate(extended(earlier, lane_of), axis=1)
    )
    return both[:count, :LANES] + (both[:count, LANES:] + both[count:, :LANES])


def carry(rows, following):
    count = rows.shape[0]
    both = dot_t(
        jnp.concatenate(split(rows), axis=0), jnp.concatenate(extended(following), axis=0)
    )
    return both[:count, :LANES] + (both[:count, LANES:] + both[count:, :LANES])


def columns(rows, n):
    count, width = rows.shape
    if width < n:
        rows = jnp.pad(rows, ((0, 0), (0, n - width)))
    turned = jnp.transpose(rows)
    if count < LANES - n:
        turned = jnp.pad(turned, ((0, 0), (0, LANES - n - count)))
    return turned


def with_offsets(matrix, offsets):
    return jnp.concatenate([matrix, offsets[: matrix.shape[0]]], axis=1)


def rounds(maps, count, size=1):
    at = 0
    while count > 2:
        end = at + count
        for k in range(count // 2):
            maps[end + k] = compose(maps[at + 2 * k + 1], maps[at + 2 * k], (2 * k + 1) * size)
        at, count, size = end, count // 2, 2 * size
    return compose(maps[at + 1], maps[at], size)


def lanes_of(shape):
    return lax.broadcasted_iota(jnp.int32, shape, 1)


def packed(total, rows):
    n = total.shape[0]
    body, spare = 3 * n // 4, n // 4
    bottom = total[body:]
    side = jnp.concatenate(
        [pltpu.roll(bottom, (n - 32 * c) % LANES, 1) if 32 * c != n else bottom for c in range(3)],
        axis=0,
    )
    top = jnp.where(lanes_of(side.shape) < n, total[:body], side)
    offset = jnp.transpose(total)[n : n + 1]
    tail = jnp.concatenate([offset, rows, jnp.zeros((7 - rows.shape[0], n), f32)], axis=0)
    return top, jnp.pad(tail, ((0, 0), (0, LANES - n)))


def unpacked(lines, offset):
    body = lines.shape[0]
    spare = body // 3
    n = body + spare
    lane = lanes_of((spare, LANES))
    bottom = offset[body:]
    for c in range(3):
        part = pltpu.roll(lines[spare * c : spare * (c + 1)], (32 * c - n) % LANES, 1)
        bottom = jnp.where(lane // 32 == c, part, bottom)
    top = jnp.where(lanes_of(lines.shape) < n, lines, offset[:body])
    return jnp.concatenate([top, bottom], axis=0)


def summary_kernel(a_hbm, d_hbm, x_hbm, out_ref, a_ref, d_ref, x_ref, maps, sems):
    steps, n = d_ref.shape
    parts = 2
    size = steps // parts
    small = [
        pltpu.make_async_copy(d_hbm, d_ref, sems.at[parts]),
        pltpu.make_async_copy(x_hbm, x_ref, sems.at[parts + 1]),
    ]
    blocks = []
    for c in range(parts):
        part = pl.ds(c * size, size)
        blocks.append(pltpu.make_async_copy(a_hbm.at[part], a_ref.at[part], sems.at[c]))
    for copy in small[:1] + blocks + small[1:]:
        copy.start()
    small[0].wait()
    offsets = columns(d_ref[...], n)
    for c in range(parts):
        blocks[c].wait()
        for t in range(c * size, (c + 1) * size, 2):
            pair = [with_offsets(a_ref[k], offsets) for k in (t, t + 1)]
            maps[t // 2] = compose(pair[1], pair[0], t + 1)
    total = rounds(maps, steps // 2, 2)
    small[1].wait()
    top, tail = packed(total, x_ref[...])
    for j in range(out_ref.shape[0]):
        out_ref[j, : top.shape[0]] = top
        out_ref[j, top.shape[0] :] = tail


def prefix_kernel(i_ref, a_ref, d_ref, k_ref, f_ref, out_ref, maps, rows_ref):
    steps, m, n = k_ref.shape
    feeds = columns(f_ref[...], n)
    offsets = columns(d_ref[...], n)
    for t in range(steps):
        maps[t] = with_offsets(a_ref[t], offsets)
    rounds(maps, steps)
    row, lane = (lax.broadcasted_iota(jnp.int32, (n, LANES), d) for d in (0, 1))
    unit = jnp.where(row == lane, 1.0, 0.0).astype(f32)

    def put(t, value):
        rows_ref[pl.ds(t, n, stride=steps)] = value

    def get(t):
        return rows_ref[pl.ds(t, n, stride=steps)]

    put(0, unit)
    size = steps
    while size > 1:
        size //= 2
        at = 2 * steps - 2 * (steps // size)
        put(size, maps[at])
        for t in range(2 * size, steps, 2 * size):
            put(t + size, compose(maps[at + t // size], get(t), t))
    for t in range(steps):
        gain = with_offsets(-k_ref[t], feeds)
        rows_ref[pl.ds(n * steps + t, m, stride=steps)] = compose(gain, get(t), t)
    turned = [pl.multiple_of((i_ref[0] + k) % 4 * steps, steps) for k in range(4)]
    for at in range(0, (n + m) * steps, LANES):
        high, low = split(rows_ref[at : at + LANES])
        for k in range(4):
            part = slice(k * steps, (k + 1) * steps)
            out_ref[pl.ds(at + turned[k], steps), :LANES] = high[part]
            out_ref[pl.ds(at + turned[k], steps), LANES:] = low[part]


def heads_of(r_ref, body, orders):
    return [
        jnp.concatenate([r_ref[j, body + k : body + k + 1] for j in order], axis=0)
        for k, order in enumerate(orders)
    ]


def unpack(r_ref, maps):
    count, lines, _ = r_ref.shape
    n = maps.shape[1]
    body = lines - 8
    heads = heads_of(r_ref, body, [range(count), ALONG, ALONG])
    offsets = with_offsets(jnp.zeros((n, n), f32), columns(heads[0][:, :n], n))
    for j in range(count):
        maps[j] = unpacked(r_ref[j, :body], offsets)
    return heads[1:]


def group_kernel(i_ref, r_ref, out_ref, inner_ref, maps):
    count, n = r_ref.shape[0], maps.shape[1]
    index = i_ref[0]
    starts = unpack(r_ref, maps)
    total = rounds(maps, count)
    row, lane = (lax.broadcasted_iota(jnp.int32, (n, LANES), d) for d in (0, 1))
    held = jnp.where(row == lane, 1.0, 0.0).astype(f32)
    bit = count // 2
    while bit:
        pair = index // (2 * bit)
        at = 2 * count - 2 * (count // bit) + pair * 2
        held = jnp.where((index & bit) != 0, compose(maps[at], held, pair * 2 * bit), held)
        bit //= 2
    inner_ref[...] = held
    for j in range(out_ref.shape[0]):
        out_ref[j, :n] = total
        for s in range(2):
            out_ref[j, n + s * count : n + (s + 1) * count] = starts[s]


def apply_kernel(i_ref, rows_ref, inner_ref, maps_ref, out_ref):
    n = inner_ref.shape[0]
    row = i_ref[0]
    outer = rows_ref.shape[0]
    size = (rows_ref.shape[1] - n) // 2
    start = jnp.concatenate(
        [rows_ref[k, n + s * size : n + (s + 1) * size] for s in (0, 1) for k in range(outer)],
        axis=0,
    )
    lane = lanes_of(start.shape)
    start = jnp.where(lane < n, start, jnp.where(lane == n, 1.0, 0.0))
    first = jnp.where(row > 1, compose(rows_ref[1, :n], rows_ref[0, :n]), rows_ref[0, :n])
    second = jnp.where(row > 2, compose(inner_ref[...], rows_ref[2, :n]), inner_ref[...])
    start = jnp.where(row > 0, carry(start, first), start)
    xh, xl = split(carry(start, second))
    x = jnp.concatenate(
        [jnp.concatenate([xh, xh], axis=1), jnp.concatenate([xl, jnp.zeros_like(xl)], axis=1)],
        axis=0,
    )
    count = maps_ref.shape[0] // LANES
    first = count * 2 // 3
    rest = count - first
    for q in range(0, count, 2):
        value = dot_t(x, maps_ref[q * LANES : (q + 2) * LANES])
        value = value[:64] + value[64:]
        for p in (0, 1):
            for s in (0, 1):
                line = s * first + q + p if q < first else 2 * first + s * rest + q + p - first
                for k in range(outer):
                    own = slice(32 * s + size * k, 32 * s + size * (k + 1))
                    place = pl.ds(2 * count * ACROSS.index(k) + line, size, stride=2 * count * outer)
                    out_ref[place] = value[own, p * LANES : (p + 1) * LANES]


def order_kernel(r_ref, states_hbm, controls_hbm, tile_ref, sems):
    lines = r_ref.shape[1]
    lane = lanes_of((lines, LANES)) // 32
    cut = states_hbm.shape[0]
    copies = []
    for g in range(8):
        parts = [
            r_ref[ALONG.index((4 * g + b) % 8) * 4 + ACROSS.index(g // 2)] for b in range(4)
        ]
        for a in range(4):
            value = parts[0]
            for b in range(1, 4):
                value = jnp.where(lane == (a + b) % 4, parts[b], value)
            if a:
                value = pltpu.roll(value, LANES - 32 * a, 1)
            tile_ref[g, pl.ds(a, lines, stride=4)] = value
        across = pl.ds(g * LANES, LANES)
        for k, (rows, to) in enumerate(
            ((pl.ds(0, cut), states_hbm), (pl.ds(cut, 4 * lines - cut), controls_hbm))
        ):
            copies.append(
                pltpu.make_async_copy(tile_ref.at[g, rows], to.at[:, across], sems.at[2 * g + k])
            )
            copies[-1].start()
    for copy in copies:
        copy.wait()


VMEM = pl.BlockSpec(memory_space=pltpu.VMEM)
SMEM = pl.BlockSpec(memory_space=pltpu.SMEM)
HBM = pl.BlockSpec(memory_space=pltpu.HBM)


def call(kernel, outs, ins, to=VMEM, scratch=(), flops=0, limit=LIMIT):
    many = isinstance(outs, (list, tuple))
    return pl.pallas_call(
        kernel,
        out_shape=outs,
        in_specs=ins,
        out_specs=[to] * len(outs) if many else to,
        scratch_shapes=list(scratch),
        compiler_params=pltpu.CompilerParams(vmem_limit_bytes=limit),
        cost_estimate=pl.CostEstimate(flops=flops, bytes_accessed=4000000, transcendentals=0),
    )


def body(closed_loop, gains, feedforward, drift_terms, initial_states):
    steps, n, _ = closed_loop.shape
    m = gains.shape[1]
    blocks = lax.axis_size("tm")
    inner, outer = 8, blocks // 8
    shape = jax.ShapeDtypeStruct
    index = lax.axis_index("tm").astype(jnp.int32).reshape(1)
    at_inner, at_outer = index % inner, index // inner
    near = [[k * inner + j for j in range(inner)] for k in range(outer)]
    far = [[k * inner + j for k in range(outer)] for j in range(inner)]
    semaphores = pltpu.SemaphoreType.DMA

    payload = call(
        summary_kernel,
        shape((inner, 3 * n // 4 + 8, LANES), f32),
        [HBM] * 3,
        scratch=[
            pltpu.VMEM((steps, n, n), f32),
            pltpu.VMEM((steps, n), f32),
            pltpu.VMEM((2, n), f32),
            pltpu.VMEM((steps, n, LANES), f32),
            semaphores((6,)),
        ],
        flops=300_000_000,
        limit=60 * 1024 * 1024,
    )(closed_loop, drift_terms, jnp.transpose(initial_states))
    gathered = lax.all_to_all(payload, "tm", 0, 0, tiled=True, axis_index_groups=near)

    rows = (n + m) * steps
    local = call(
        prefix_kernel,
        shape((rows, 2 * LANES), bf16),
        [SMEM] + [VMEM] * 4,
        scratch=[
            pltpu.VMEM((2 * steps, n, LANES), f32),
            pltpu.VMEM((rows, LANES), f32),
        ],
        flops=500_000_000,
    )(index, closed_loop, drift_terms, gains, feedforward)
    gathered, local, at_inner, at_outer = lax.optimization_barrier(
        (gathered, local, at_inner, at_outer)
    )

    group, before = call(
        group_kernel,
        [shape((outer, n + 2 * inner, LANES), f32), shape((n, LANES), f32)],
        [SMEM, VMEM],
        scratch=[pltpu.VMEM((2 * inner, n, LANES), f32)],
        flops=150_000_000,
    )(at_inner, gathered)
    across = lax.all_to_all(group, "tm", 0, 0, tiled=True, axis_index_groups=far)

    lines = 2 * rows // LANES
    sent = call(
        apply_kernel,
        shape((blocks * lines, LANES), f32),
        [SMEM] + [VMEM] * 3,
        flops=300_000_000,
    )(at_outer, across, before, local)
    moved = lax.all_to_all(
        sent.reshape(blocks, lines, LANES),
        "tm",
        0,
        0,
        tiled=True,
        axis_index_groups=[[k * inner + j for j in ALONG for k in ACROSS]],
    )
    states, controls = call(
        order_kernel,
        [shape((2 * n, blocks * steps), f32), shape((2 * m, blocks * steps), f32)],
        [VMEM],
        to=HBM,
        scratch=[pltpu.VMEM((8, 4 * lines, LANES), f32), semaphores((16,))],
        flops=1_000_000,
    )(moved)
    return states.reshape(2, n, -1), controls.reshape(2, m, -1)


def solution(mesh):
    return jax.shard_map(
        body,
        mesh=mesh,
        in_specs=(
            P("tm", None, None),
            P("tm", None, None),
            P("tm", None),
            P("tm", None),
            P(None, ("tm", "scen")),
        ),
        out_specs=(P(("tm", "scen"), None, None), P(("tm", "scen"), None, None)),
        check_vma=False,
    )
```
